32 devices in a mesh: cfg: 2 (over y), ta: 8 (over z, x), sa: 2 (over core).
Axes of the slice: x: 2, y: 2, z: 4, core: 2. Of those that a mesh axis runs over, the one named last changes fastest.
Arguments:
- forward: bfloat16 [32, 2, 256, 2, 256], P(('cfg', 'ta'), 'sa'), parts along dimension 0, may hold values from -6 to 6
- backward: bfloat16 [4, 16, 256, 2, 256], P(('cfg', 'sa'), 'ta'), parts along dimension 0, may hold values from -6 to 6
- sink_bank: bfloat16 [32, 9, 256, 2, 256], P(('cfg', 'ta'), None, 'sa'), parts along dimension 0, may hold values from -0.25 to 0.25
- source_bank: bfloat16 [4, 9, 256, 2, 256], P(('cfg', 'sa'), None, 'ta'), parts along dimension 0, may hold values from -0.25 to 0.25
- op_mom: int32 [4], replicated, may hold values from 0 to 2
- op_disp: int32 [4], replicated, may hold values from 0 to 2
Outputs:
- correlator: float32 [32, 2, 2, 4, 4], P(('cfg', 'ta'), 'sa'), parts along dimension 0
The draws below stay inside these ranges and needn't reach their ends.
There are 2 independent parts, one for each index of `cfg`. The reference program is written for one: setup_inputs(seed, part) draws one part's arguments, and reference() takes and returns one part's arrays. A program takes and returns all parts, laid end to end along the dimension named above; an argument that names none is the same for every part. Nothing has to cross between parts.
All inputs are finite; a program needn't handle non-finite values.
Results may differ from the reference program's by a relative error of at most 0.0029.
Values may be sent and summed in bfloat16 or wider, within the bound.
No kernel may reach another device: no remote copies, remote signals or barrier semaphores. Data moves between devices by JAX's collectives and lax.ppermute only.
A program may use at most 64 MiB of HBM per device.

```python
import jax
import jax.numpy as jnp
from jax import lax

P_SIZE = 256
NOP = 4
NMOM = 3
NDISP = 3
NBANK = 9
NT = 16
NS = 2


def place_ends(values, own_key, low, largest):
    index_at = [jax.random.randint(jax.random.fold_in(own_key, axis), (), 0, length) for axis, length in enumerate(values.shape)]
    main_axis = values.shape.index(max(values.shape))
    neighbour = index_at[:main_axis] + [(index_at[main_axis] + 1) % values.shape[main_axis]] + index_at[main_axis + 1:]
    return values.at[tuple(index_at)].set(low).at[tuple(neighbour)].set(largest)


def level_of(stream_key, shape, shards, low, high):
    factor_of = 1.0
    for axis_at, shards_of in shards:
        draws = jax.random.uniform(jax.random.fold_in(jax.random.fold_in(stream_key, 6), axis_at), (shards_of,), jnp.float32, low / len(shards), high / len(shards))
        factor_of = factor_of * jnp.repeat(jnp.exp(draws), shape[axis_at] // shards_of).reshape((-1,) + (1,) * (len(shape) - 1 - axis_at))
    return factor_of


def normal_values(stream_key, shape, width, limit, cuts=(), kind=jnp.bfloat16):
    array = jax.random.normal(stream_key, shape, jnp.float32) * width
    if len(cuts) > 0:
        array = level_of(stream_key, shape, cuts, -0.22, 0.18) * array
    return jnp.clip(array, min=-limit, max=limit).astype(kind)


def setup_inputs(seed: int = 0, part: int = 0) -> dict:
    key_of = jax.random.split(jax.random.key(seed), 7)
    part_splits = jax.random.split(jax.random.fold_in(key_of[6], part), 7)
    return {
        "forward": normal_values(part_splits[0], (NT, NS, P_SIZE, 2, P_SIZE), 1.0, 6.0, ((0, 8), (1, 2))),
        "backward": normal_values(part_splits[1], (NS, NT, P_SIZE, 2, P_SIZE), 1.0, 6.0, ((0, 2), (1, 8))),
        "sink_bank": normal_values(part_splits[2], (NT, NBANK, P_SIZE, 2, P_SIZE), (2 * P_SIZE) ** -0.5, 0.25, ((0, 8), (2, 2))),
        "source_bank": normal_values(part_splits[3], (NS, NBANK, P_SIZE, 2, P_SIZE), (2 * P_SIZE) ** -0.5, 0.25, ((0, 2), (2, 8))),
        "op_mom": place_ends(jax.random.randint(key_of[4], (NOP,), 0, NMOM), jax.random.fold_in(key_of[4], 1), 0, NMOM - 1).astype(jnp.int32),
        "op_disp": place_ends(jax.random.randint(key_of[5], (NOP,), 0, NDISP), jax.random.fold_in(key_of[5], 1), 0, NDISP - 1).astype(jnp.int32),
    }


def complex_product(left, right):
    count = left.shape[0]
    height = left.shape[1]
    left_real = left[:, :, 0, :].reshape(count * height, -1)
    left_imag = left[:, :, 1, :].reshape(count * height, -1)
    right_real = right[:, 0, :]
    right_imag = right[:, 1, :]
    real_part = jnp.dot(left_real, right_real, preferred_element_type=jnp.float32) - jnp.dot(left_imag, right_imag, preferred_element_type=jnp.float32)
    imag_part = jnp.dot(left_real, right_imag, preferred_element_type=jnp.float32) + jnp.dot(left_imag, right_real, preferred_element_type=jnp.float32)
    return jnp.stack([real_part, imag_part], axis=1).reshape(count, height, 2, -1)


def reference(forward, backward, sink_bank, source_bank, op_mom, op_disp):
    wanted = (op_mom * NDISP + op_disp).astype(jnp.int32)
    sink_ops = jnp.take(sink_bank, wanted, axis=1)
    source_ops = jnp.take(source_bank, wanted, axis=1)
    back_by_time = jnp.swapaxes(backward, 0, 1)

    def one_time(items):
        ops_here, forward_here, back_here = items
        blocks = []
        for source in range(NS):
            product = complex_product(ops_here, forward_here[source]).astype(jnp.bfloat16)
            reverse = complex_product(source_ops[source], back_here[source])
            paired = jnp.einsum("aicj,bjdi->abcd", product.astype(jnp.float32), reverse, precision=lax.Precision.HIGHEST)
            real_trace = paired[:, :, 0, 0] - paired[:, :, 1, 1]
            imag_trace = paired[:, :, 0, 1] + paired[:, :, 1, 0]
            blocks.append(jnp.stack([real_trace, imag_trace], axis=0) / P_SIZE)
        return jnp.stack(blocks, axis=0)

    return lax.map(one_time, (sink_ops, forward, back_by_time))
```

```python
import functools

import jax
import jax.numpy as jnp
from jax import lax
from jax.experimental import pallas as pl
from jax.experimental.pallas import tpu as pltpu
from jax.sharding import PartitionSpec as P

NDISP = 3
VMEM_LIMIT = 40 * 1024 * 1024
WHOLE = pl.BlockSpec(memory_space=pltpu.VMEM)
SCALARS = pl.BlockSpec(memory_space=pltpu.SMEM)


def chosen_entries(bank, wanted):
    picked = [
        lax.dynamic_index_in_dim(bank, wanted[a], axis=1, keepdims=False)
        for a in range(wanted.shape[0])
    ]
    return jnp.stack(picked, axis=1)


def planar(matrices):
    return jnp.swapaxes(matrices, 1, 2)


def snake_hops(count, hop):
    walk = list(range(0, count, 2)) + list(range(1, count, 2))[::-1]
    return [(walk[k], walk[(k + hop) % count]) for k in range(count)]


def sink_kernel(half_ref, forward_ref, own_ref, other_ref, out_ref):
    mine = half_ref[0]
    for t in range(forward_ref.shape[0]):
        real = forward_ref[t, 0].T
        imag = forward_ref[t, 1].T
        for_real = jnp.concatenate([real, -imag], axis=1)
        for_imag = jnp.concatenate([imag, real], axis=1)
        left = jnp.concatenate([for_real, for_imag], axis=0)
        for ops_ref, half in ((own_ref, mine), (other_ref, 1 - mine)):
            out_ref[t, half] = lax.dot_general(
                left, ops_ref[t], (((1,), (1,)), ((), ())), preferred_element_type=jnp.float32
            ).astype(jnp.bfloat16)


def trace_kernel(n_halves, last, nop, rows, *refs):
    place_ref, product_ref, back_ref = refs[:3]
    pieces = []
    at = 3
    for halves in n_halves:
        pieces.append(refs[at : at + halves])
        at += halves
    before_ref = refs[at] if at < len(refs) - 1 else None
    out_ref = refs[-1]
    times = product_ref.shape[0]
    order = back_ref.shape[2]
    totals = [None if before_ref is None else before_ref[t] for t in range(times)]
    for k, parts in enumerate(pieces):
        if len(parts) == 1:
            height = parts[0].shape[0] // 2
            real, imag = parts[0][:height], parts[0][height:]
        else:
            real, imag = parts[0][...], parts[1][...]
        for_real = jnp.concatenate([real, -imag], axis=1)
        for_imag = jnp.concatenate([imag, real], axis=1)
        left = jnp.concatenate([for_real, for_imag], axis=0)
        start = pl.multiple_of(place_ref[k] * rows, rows)
        for t in range(times):
            reverse = jnp.dot(left, back_ref[t], preferred_element_type=jnp.float32)
            high = reverse.astype(jnp.bfloat16)
            low = (reverse - high.astype(jnp.float32)).astype(jnp.bfloat16)
            blocks = []
            for part in range(2):
                two = [
                    product_ref[t, half, pl.ds(pl.multiple_of(part * order + start, rows), rows), :]
                    for half in range(2)
                ]
                width = two[0].shape[1] // nop
                for a in range(nop):
                    blocks.append(
                        jnp.concatenate([x[:, a * width : (a + 1) * width] for x in two], axis=1)
                    )
            sink = jnp.concatenate(blocks, axis=0)
            nt = (((1,), (1,)), ((), ()))
            added = lax.dot_general(sink, high, nt, preferred_element_type=jnp.float32)
            added += lax.dot_general(sink, low, nt, preferred_element_type=jnp.float32)
            totals[t] = added if totals[t] is None else totals[t] + added
    if not last:
        for t in range(times):
            out_ref[t] = totals[t]
        return
    side = totals[0].shape[0]
    row_at = lax.broadcasted_iota(jnp.int32, (side, side), 0)
    column_at = lax.broadcasted_iota(jnp.int32, (side, side), 1)
    same = lax.rem(row_at, rows) == lax.rem(column_at, rows)
    groups = side // rows
    in_group = (
        lax.broadcasted_iota(jnp.int32, (side, groups), 0) // rows
        == lax.broadcasted_iota(jnp.int32, (side, groups), 1)
    ).astype(jnp.float32)
    for t in range(times):
        kept = jnp.where(same, totals[t], 0.0)
        summed = kept.reshape(groups, rows, side).sum(axis=1)
        paired = jnp.dot(
            summed, in_group, preferred_element_type=jnp.float32, precision=lax.Precision.HIGHEST
        )
        out_ref[t, 0] = (paired[:nop, :nop] - paired[nop:, nop:]) / order
        out_ref[t, 1] = (paired[:nop, nop:] + paired[nop:, :nop]) / order


def traces(product, back, pieces, places, nop, rows, before=None, last=False):
    times = product.shape[0]
    side = 2 * nop * rows
    operands = [places, product, back]
    for parts in pieces:
        operands += list(parts)
    if before is not None:
        operands.append(before)
    shape = (times, 2, nop, nop) if last else (times, side, side)
    order = back.shape[2]
    flops = 2 * times * len(pieces) * side * (2 * order * order + 2 * side * order)
    return pl.pallas_call(
        functools.partial(trace_kernel, tuple(len(p) for p in pieces), last, nop, rows),
        out_shape=jax.ShapeDtypeStruct(shape, jnp.float32),
        in_specs=[SCALARS] + [WHOLE] * (len(operands) - 1),
        out_specs=WHOLE,
        compiler_params=pltpu.CompilerParams(vmem_limit_bytes=VMEM_LIMIT),
        cost_estimate=pl.CostEstimate(flops=flops, bytes_accessed=4 * 1024 * 1024, transcendentals=0),
        name="traces_last" if last else "traces",
    )(*operands)


def per_device(forward, backward, sink_bank, source_bank, op_mom, op_disp, n_times):
    wanted = op_mom * NDISP + op_disp
    nop = wanted.shape[0]
    order = forward.shape[2]
    times = forward.shape[0]
    own_rows = source_bank.shape[2]
    me = lax.axis_index("ta")
    half = lax.axis_index("sa")

    source = jnp.transpose(chosen_entries(source_bank, wanted)[0], (2, 0, 1, 3)).reshape(-1, order)

    sink_own = chosen_entries(sink_bank, wanted).reshape(times, -1, 2 * order)
    sink_other = lax.ppermute(sink_own, "sa", [(0, 1), (1, 0)])
    product = pl.pallas_call(
        sink_kernel,
        out_shape=jax.ShapeDtypeStruct((times, 2, 2 * order, sink_own.shape[1]), jnp.bfloat16),
        in_specs=[SCALARS, WHOLE, WHOLE, WHOLE],
        out_specs=WHOLE,
        compiler_params=pltpu.CompilerParams(vmem_limit_bytes=VMEM_LIMIT),
        cost_estimate=pl.CostEstimate(
            flops=2 * times * 2 * order * 2 * order * order * nop,
            bytes_accessed=5 * 1024 * 1024,
            transcendentals=0,
        ),
        name="sink_product",
    )(half.reshape(1).astype(jnp.int32), planar(forward[:, 0]), sink_own, sink_other)
    back = planar(backward[0]).reshape(times, 2 * order, order)

    rows = order // (2 * nop)
    if own_rows == rows:
        def hop(array, k):
            return lax.ppermute(array, "ta", snake_hops(n_times, k))

        walk = jnp.asarray([a for a, _ in snake_hops(n_times, 1)], jnp.int32)
        spot = jnp.argmax(walk == me).astype(jnp.int32)

        def places(*offsets):
            return jnp.stack([walk[(spot + k) % n_times] for k in offsets])

        cut = source.shape[0] // 2
        up1, down1 = hop(source, 1), hop(source, -1)
        up2, down2 = hop(source, 2), hop(source, -2)
        up3, down3 = hop(up2, 1), hop(down2, -1)
        up4, down4 = hop(up2[:cut], 2), hop(down2[cut:], -2)
        first = traces(
            product, back, [(source,), (up1,), (down1,), (up2,), (down2,)], places(0, -1, 1, -2, 2), nop, rows
        )
        result = traces(
            product, back, [(up3,), (down3,), (up4, down4)], places(-3, 3, 4), nop, rows, before=first, last=True
        )
    else:
        whole = lax.all_gather(source.reshape(2, nop, own_rows, order), "ta", axis=2, tiled=True)
        pieces = [
            (whole[:, :, k * rows : (k + 1) * rows].reshape(-1, order),) for k in range(order // rows)
        ]
        result = traces(
            product, back, pieces, jnp.arange(order // rows, dtype=jnp.int32), nop, rows, last=True
        )
    return result[:, None]


def solution(mesh):
    placed = (
        P(("cfg", "ta"), "sa", None, None, None),
        P(("cfg", "sa"), "ta", None, None, None),
        P(("cfg", "ta"), None, "sa", None, None),
        P(("cfg", "sa"), None, "ta", None, None),
        P(),
        P(),
    )
    return jax.shard_map(
        functools.partial(per_device, n_times=mesh.shape["ta"]),
        mesh=mesh,
        in_specs=placed,
        out_specs=P(("cfg", "ta"), "sa", None, None, None),
        check_vma=False,
    )
```

```python
import functools

import jax
import jax.numpy as jnp
from jax import lax
from jax.experimental import pallas as pl
from jax.experimental.pallas import tpu as pltpu
from jax.sharding import PartitionSpec as P

NDISP = 3
VMEM_LIMIT = 40 * 1024 * 1024
WHOLE = pl.BlockSpec(memory_space=pltpu.VMEM)
SCALARS = pl.BlockSpec(memory_space=pltpu.SMEM)


def select_kernel(mom_ref, disp_ref, bank_ref, out_ref, arrived):
    copies = []
    for a in range(out_ref.shape[1]):
        entry = mom_ref[a] * NDISP + disp_ref[a]
        copies.append(pltpu.make_async_copy(bank_ref.at[:, entry], out_ref.at[:, a], arrived.at[a]))
        copies[-1].start()
    for copy in copies:
        copy.wait()


def chosen_entries(bank, op_mom, op_disp, name):
    nop = op_mom.shape[0]
    shape = (bank.shape[0], nop) + bank.shape[2:]
    return pl.pallas_call(
        select_kernel,
        out_shape=jax.ShapeDtypeStruct(shape, bank.dtype),
        in_specs=[SCALARS, SCALARS, pl.BlockSpec(memory_space=pl.ANY)],
        out_specs=WHOLE,
        scratch_shapes=[pltpu.SemaphoreType.DMA((nop,))],
        compiler_params=pltpu.CompilerParams(vmem_limit_bytes=VMEM_LIMIT),
        name=name,
    )(op_mom, op_disp, bank)


def planar(matrices):
    return jnp.swapaxes(matrices, 1, 2)


def snake_at(spot, count):
    return jnp.where(2 * spot < count, 2 * spot, 2 * (count - 1 - spot) + 1)


def snake_spot(index, count):
    return jnp.where(lax.rem(index, 2) == 0, index // 2, count - 1 - index // 2)


def snake_hops(count, hop):
    walk = list(range(0, count, 2)) + list(range(1, count, 2))[::-1]
    return [(walk[k], walk[(k + hop) % count]) for k in range(count)]


def sink_kernel(forward_ref, own_ref, other_ref, out_ref):
    mine = lax.axis_index("sa")
    for t in range(forward_ref.shape[0]):
        real = forward_ref[t, 0].T
        imag = forward_ref[t, 1].T
        for_real = jnp.concatenate([real, -imag], axis=1)
        for_imag = jnp.concatenate([imag, real], axis=1)
        left = jnp.concatenate([for_real, for_imag], axis=0)
        for ops_ref, half in ((own_ref, mine), (other_ref, 1 - mine)):
            out_ref[t, half] = lax.dot_general(
                left, ops_ref[t], (((1,), (1,)), ((), ())), preferred_element_type=jnp.float32
            ).astype(jnp.bfloat16)


def trace_kernel(n_halves, spots, count, last, nop, rows, *refs):
    product_ref, back_ref = refs[:2]
    own_spot = None if count is None else snake_spot(lax.axis_index("ta"), count)
    pieces = []
    at = 2
    for halves in n_halves:
        pieces.append(refs[at : at + halves])
        at += halves
    before_ref = refs[at] if at < len(refs) - 1 else None
    out_ref = refs[-1]
    times = product_ref.shape[0]
    order = back_ref.shape[2]
    totals = [None if before_ref is None else before_ref[t] for t in range(times)]
    for k, parts in enumerate(pieces):
        if len(parts) == 1:
            height = parts[0].shape[0] // 2
            real, imag = parts[0][:height], parts[0][height:]
        else:
            real, imag = parts[0][...], parts[1][...]
        for_real = jnp.concatenate([real, -imag], axis=1)
        for_imag = jnp.concatenate([imag, real], axis=1)
        left = jnp.concatenate([for_real, for_imag], axis=0)
        if own_spot is None:
            start = spots[k] * rows
        else:
            spot = lax.rem(own_spot + (spots[k] + count), count)
            start = pl.multiple_of(snake_at(spot, count) * rows, rows)
        for t in range(times):
            reverse = jnp.dot(left, back_ref[t], preferred_element_type=jnp.float32)
            high = reverse.astype(jnp.bfloat16)
            low = (reverse - high.astype(jnp.float32)).astype(jnp.bfloat16)
            blocks = []
            for part in range(2):
                two = [
                    product_ref[t, half, pl.ds(part * order + start, rows), :]
                    for half in range(2)
                ]
                width = two[0].shape[1] // nop
                for a in range(nop):
                    blocks.append(
                        jnp.concatenate([x[:, a * width : (a + 1) * width] for x in two], axis=1)
                    )
            sink = jnp.concatenate(blocks, axis=0)
            nt = (((1,), (1,)), ((), ()))
            added = lax.dot_general(sink, high, nt, preferred_element_type=jnp.float32)
            added += lax.dot_general(sink, low, nt, preferred_element_type=jnp.float32)
            totals[t] = added if totals[t] is None else totals[t] + added
    if not last:
        for t in range(times):
            out_ref[t] = totals[t]
        return
    side = totals[0].shape[0]
    row_at = lax.broadcasted_iota(jnp.int32, (side, side), 0)
    column_at = lax.broadcasted_iota(jnp.int32, (side, side), 1)
    same = lax.rem(row_at, rows) == lax.rem(column_at, rows)
    groups = side // rows
    in_group = (
        lax.broadcasted_iota(jnp.int32, (side, groups), 0) // rows
        == lax.broadcasted_iota(jnp.int32, (side, groups), 1)
    ).astype(jnp.float32)
    for t in range(times):
        kept = jnp.where(same, totals[t], 0.0)
        summed = kept.reshape(groups, rows, side).sum(axis=1)
        paired = jnp.dot(
            summed, in_group, preferred_element_type=jnp.float32, precision=lax.Precision.HIGHEST
        )
        out_ref[t, 0] = (paired[:nop, :nop] - paired[nop:, nop:]) / order
        out_ref[t, 1] = (paired[:nop, nop:] + paired[nop:, :nop]) / order


def traces(product, back, pieces, spots, count, nop, rows, before=None, last=False):
    times = product.shape[0]
    side = 2 * nop * rows
    operands = [product, back]
    for parts in pieces:
        operands += list(parts)
    if before is not None:
        operands.append(before)
    shape = (times, 2, nop, nop) if last else (times, side, side)
    order = back.shape[2]
    flops = 2 * times * len(pieces) * side * (2 * order * order + 2 * side * order)
    return pl.pallas_call(
        functools.partial(trace_kernel, tuple(len(p) for p in pieces), spots, count, last, nop, rows),
        out_shape=jax.ShapeDtypeStruct(shape, jnp.float32),
        in_specs=[WHOLE] * len(operands),
        out_specs=WHOLE,
        compiler_params=pltpu.CompilerParams(vmem_limit_bytes=VMEM_LIMIT),
        cost_estimate=pl.CostEstimate(flops=flops, bytes_accessed=4 * 1024 * 1024, transcendentals=0),
        name="traces_last" if last else "traces",
    )(*operands)


def per_device(forward, backward, sink_bank, source_bank, op_mom, op_disp, n_times):
    nop = op_mom.shape[0]
    order = forward.shape[2]
    times = forward.shape[0]
    own_rows = source_bank.shape[2]

    source = jnp.transpose(chosen_entries(source_bank, op_mom, op_disp, "source_rows")[0], (2, 0, 1, 3)).reshape(-1, order)

    sink_own = chosen_entries(sink_bank, op_mom, op_disp, "sink_rows").reshape(times, -1, 2 * order)
    sink_other = lax.ppermute(sink_own, "sa", [(0, 1), (1, 0)])
    product = pl.pallas_call(
        sink_kernel,
        out_shape=jax.ShapeDtypeStruct((times, 2, 2 * order, sink_own.shape[1]), jnp.bfloat16),
        in_specs=[WHOLE, WHOLE, WHOLE],
        out_specs=WHOLE,
        compiler_params=pltpu.CompilerParams(vmem_limit_bytes=VMEM_LIMIT),
        cost_estimate=pl.CostEstimate(
            flops=2 * times * 2 * order * 2 * order * order * nop,
            bytes_accessed=5 * 1024 * 1024,
            transcendentals=0,
        ),
        name="sink_product",
    )(planar(forward[:, 0]), sink_own, sink_other)
    back = planar(backward[0]).reshape(times, 2 * order, order)

    rows = order // (2 * nop)
    if own_rows == rows:
        def hop(array, k):
            return lax.ppermute(array, "ta", snake_hops(n_times, k))

        cut = source.shape[0] // 2
        up1, down1 = hop(source, 1), hop(source, -1)
        up2, down2 = hop(source, 2), hop(source, -2)
        up3, down3 = hop(up2, 1), hop(down2, -1)
        up4, down4 = hop(up2[:cut], 2), hop(down2[cut:], -2)
        first = traces(
            product, back, [(source,), (up1,), (down1,), (up2,), (down2,)], (0, -1, 1, -2, 2), n_times, nop, rows
        )
        result = traces(
            product, back, [(up3,), (down3,), (up4, down4)], (-3, 3, 4), n_times, nop, rows, before=first, last=True
        )
    else:
        whole = lax.all_gather(source.reshape(2, nop, own_rows, order), "ta", axis=2, tiled=True)
        pieces = [
            (whole[:, :, k * rows : (k + 1) * rows].reshape(-1, order),) for k in range(order // rows)
        ]
        result = traces(
            product, back, pieces, tuple(range(order // rows)), None, nop, rows, last=True
        )
    return result[:, None]


def solution(mesh):
    placed = (
        P(("cfg", "ta"), "sa", None, None, None),
        P(("cfg", "sa"), "ta", None, None, None),
        P(("cfg", "ta"), None, "sa", None, None),
        P(("cfg", "sa"), None, "ta", None, None),
        P(),
        P(),
    )
    return jax.shard_map(
        functools.partial(per_device, n_times=mesh.shape["ta"]),
        mesh=mesh,
        in_specs=placed,
        out_specs=P(("cfg", "ta"), "sa", None, None, None),
        check_vma=False,
    )
```

```python
import functools

import jax
import jax.numpy as jnp
from jax import lax
from jax.experimental import pallas as pl
from jax.experimental.pallas import tpu as pltpu
from jax.sharding import PartitionSpec as P

NDISP = 3
VMEM_LIMIT = 40 * 1024 * 1024
WHOLE = pl.BlockSpec(memory_space=pltpu.VMEM)
IN_HBM = pl.BlockSpec(memory_space=pltpu.HBM)


def source_kernel(mom_ref, disp_ref, bank_ref, out_ref, mom, disp, bank, arrived):
    copies = [
        pltpu.make_async_copy(mom_ref, mom, arrived.at[0]),
        pltpu.make_async_copy(disp_ref, disp, arrived.at[1]),
        pltpu.make_async_copy(bank_ref, bank, arrived.at[2]),
    ]
    for copy in copies:
        copy.start()
    for copy in copies:
        copy.wait()
    for a in range(out_ref.shape[1]):
        out_ref[:, a] = bank[:, mom[a] * NDISP + disp[a]]


def chosen_source_rows(bank, op_mom, op_disp):
    nop = op_mom.shape[0]
    return pl.pallas_call(
        source_kernel,
        out_shape=pltpu.VMEM((bank.shape[0], nop) + bank.shape[2:], bank.dtype),
        in_specs=[IN_HBM] * 3,
        out_specs=WHOLE,
        scratch_shapes=[
            pltpu.SMEM((nop,), jnp.int32),
            pltpu.SMEM((nop,), jnp.int32),
            pltpu.VMEM(bank.shape, bank.dtype),
            pltpu.SemaphoreType.DMA((3,)),
        ],
        compiler_params=pltpu.CompilerParams(vmem_limit_bytes=VMEM_LIMIT),
        name="source_rows",
    )(*(pltpu.with_memory_space_constraint(x, pltpu.HBM) for x in (op_mom, op_disp, bank)))


def planar(matrices):
    return jnp.swapaxes(matrices, 1, 2)


def swap(array, mask, count):
    return lax.ppermute(array, "ta", [(k, k ^ mask) for k in range(count)])


def sink_kernel(mom_ref, disp_ref, forward_ref, own_ref, other_ref, out_ref, mom, disp, forward, rows, arrived):
    times, nop = rows.shape[:2]
    numbers = [
        pltpu.make_async_copy(mom_ref, mom, arrived.at[nop]),
        pltpu.make_async_copy(disp_ref, disp, arrived.at[nop + 1]),
    ]
    whole = pltpu.make_async_copy(forward_ref, forward, arrived.at[nop + 2])
    for copy in numbers + [whole]:
        copy.start()
    for copy in numbers:
        copy.wait()
    entries = [mom[a] * NDISP + disp[a] for a in range(nop)]
    copies = [
        pltpu.make_async_copy(own_ref.at[:, e], rows.at[:, a], arrived.at[a]) for a, e in enumerate(entries)
    ]
    for copy in copies:
        copy.start()
    whole.wait()
    lefts = []
    for t in range(times):
        parts = jnp.swapaxes(forward[t, 0], 0, 1)
        real, imag = parts[0].T, parts[1].T
        for_real = jnp.concatenate([real, -imag], axis=1)
        for_imag = jnp.concatenate([imag, real], axis=1)
        lefts.append(jnp.concatenate([for_real, for_imag], axis=0))
    mine = lax.axis_index("sa")

    def multiply(half, pick):
        for t in range(times):
            chosen = [jnp.swapaxes(pick(t, a), 0, 1) for a in range(nop)]
            right = jnp.concatenate([jnp.concatenate([x[0], x[1]], axis=1) for x in chosen], axis=0)
            out_ref[t, half] = lax.dot_general(
                lefts[t], right, (((1,), (1,)), ((), ())), preferred_element_type=jnp.float32
            ).astype(jnp.bfloat16)

    multiply(1 - mine, lambda t, a: other_ref[t, entries[a]])
    for copy in copies:
        copy.wait()
    multiply(mine, lambda t, a: rows[t, a])


def sink_products(forward, own_bank, other_bank, op_mom, op_disp):
    nop = op_mom.shape[0]
    times, order = forward.shape[0], forward.shape[2]
    return pl.pallas_call(
        sink_kernel,
        out_shape=jax.ShapeDtypeStruct((times, 2, 2 * order, nop * own_bank.shape[2]), jnp.bfloat16),
        in_specs=[IN_HBM] * 4 + [WHOLE],
        out_specs=WHOLE,
        scratch_shapes=[
            pltpu.SMEM((nop,), jnp.int32),
            pltpu.SMEM((nop,), jnp.int32),
            pltpu.VMEM(forward.shape, forward.dtype),
            pltpu.VMEM((times, nop) + own_bank.shape[2:], own_bank.dtype),
            pltpu.SemaphoreType.DMA((nop + 3,)),
        ],
        compiler_params=pltpu.CompilerParams(vmem_limit_bytes=VMEM_LIMIT),
        cost_estimate=pl.CostEstimate(
            flops=2 * times * 2 * order * 2 * order * order * nop,
            bytes_accessed=5 * 1024 * 1024,
            transcendentals=0,
        ),
        name="sink_product",
    )(
        *(pltpu.with_memory_space_constraint(x, pltpu.HBM) for x in (op_mom, op_disp, forward, own_bank)),
        other_bank,
    )


def trace_kernel(masks, known, last, nop, rows, *refs):
    product_ref, back_ref = refs[:2]
    me = 0 if known else lax.axis_index("ta")
    piece_refs = refs[2 : 2 + len(masks)]
    before_ref = refs[2 + len(masks)] if len(refs) == 4 + len(masks) else None
    out_ref = refs[-1]
    times = product_ref.shape[0]
    order = back_ref.shape[2]
    totals = [None if before_ref is None else before_ref[t] for t in range(times)]
    for mask, piece_ref in zip(masks, piece_refs):
        height = piece_ref.shape[0] // 2
        real, imag = piece_ref[:height], piece_ref[height:]
        for_real = jnp.concatenate([real, -imag], axis=1)
        for_imag = jnp.concatenate([imag, real], axis=1)
        left = jnp.concatenate([for_real, for_imag], axis=0)
        start = pl.multiple_of((me ^ mask) * rows, rows)
        for t in range(times):
            reverse = jnp.dot(left, back_ref[t], preferred_element_type=jnp.float32)
            high = reverse.astype(jnp.bfloat16)
            low = (reverse - high.astype(jnp.float32)).astype(jnp.bfloat16)
            blocks = []
            for part in range(2):
                two = [
                    product_ref[t, half, pl.ds(part * order + start, rows), :]
                    for half in range(2)
                ]
                width = two[0].shape[1] // nop
                for a in range(nop):
                    blocks.append(
                        jnp.concatenate([x[:, a * width : (a + 1) * width] for x in two], axis=1)
                    )
            sink = jnp.concatenate(blocks, axis=0)
            nt = (((1,), (1,)), ((), ()))
            added = lax.dot_general(sink, high, nt, preferred_element_type=jnp.float32)
            added += lax.dot_general(sink, low, nt, preferred_element_type=jnp.float32)
            totals[t] = added if totals[t] is None else totals[t] + added
    if not last:
        for t in range(times):
            out_ref[t] = totals[t]
        return
    side = totals[0].shape[0]
    shape = (2, nop, rows, 2 * nop * rows)
    row_part = lax.broadcasted_iota(jnp.int32, shape, 0)
    row_at = lax.broadcasted_iota(jnp.int32, shape, 2)
    column_at = lax.broadcasted_iota(jnp.int32, shape, 3)
    column_part = (column_at >= nop * rows).astype(jnp.int32)
    same = row_at == lax.rem(column_at, rows)
    sign = jnp.where(row_part == 0, 1.0, -1.0)
    weights = (
        jnp.where(same & (row_part == column_part), sign, 0.0),
        jnp.where(same & (row_part != column_part), 1.0, 0.0),
    )
    sums = []
    for t in range(times):
        table = totals[t].reshape(shape)
        for weight in weights:
            sums.append((table * weight).sum(axis=(0, 2)))
    left_over = jnp.concatenate(sums, axis=0)
    height = left_over.shape[0]
    terms = []
    for _ in range(3):
        terms.append(left_over.astype(jnp.bfloat16))
        left_over = left_over - terms[-1].astype(jnp.float32)
    of_operator = (
        lax.rem(lax.broadcasted_iota(jnp.int32, (side, nop), 0) // rows, nop)
        == lax.broadcasted_iota(jnp.int32, (side, nop), 1)
    ).astype(jnp.bfloat16)
    paired = jnp.dot(jnp.concatenate(terms, axis=0), of_operator, preferred_element_type=jnp.float32)
    paired = (paired[:height] + (paired[height : 2 * height] + paired[2 * height :])) / order
    for t in range(times):
        for part in range(2):
            at = (2 * t + part) * nop
            out_ref[t, part] = paired[at : at + nop]


def traces(product, back, pieces, nop, rows, known=False, before=None, last=False):
    times, order = product.shape[0], back.shape[2]
    side = 2 * nop * rows
    operands = [product, back, *pieces.values()] + ([] if before is None else [before])
    shape = (times, 2, nop, nop) if last else (times, side, side)
    flops = 2 * times * len(pieces) * side * (2 * order * order + 2 * side * order)
    return pl.pallas_call(
        functools.partial(trace_kernel, tuple(pieces), known, last, nop, rows),
        out_shape=jax.ShapeDtypeStruct(shape, jnp.float32),
        in_specs=[WHOLE] * len(operands),
        out_specs=WHOLE,
        compiler_params=pltpu.CompilerParams(vmem_limit_bytes=VMEM_LIMIT),
        cost_estimate=pl.CostEstimate(flops=flops, bytes_accessed=4 * 1024 * 1024, transcendentals=0),
        name="traces_last" if last else "traces",
    )(*operands)


def per_device(forward, backward, sink_bank, source_bank, op_mom, op_disp, n_times):
    nop = op_mom.shape[0]
    order = forward.shape[2]
    times = forward.shape[0]
    own_rows = source_bank.shape[2]

    source_raw = chosen_source_rows(source_bank, op_mom, op_disp)
    source = jnp.transpose(source_raw[0], (2, 0, 1, 3)).reshape(-1, order)
    other_bank = lax.ppermute(sink_bank, "sa", [(0, 1), (1, 0)])
    product = sink_products(
        forward,
        sink_bank,
        other_bank,
        op_mom,
        op_disp,
    )
    back = planar(backward[0]).reshape(times, 2 * order, order)

    rows = order // (2 * nop)
    far_mask = n_times // 2
    if own_rows == rows and n_times == 2 * far_mask and far_mask & (far_mask - 1) == 0:
        near = range(1, far_mask)
        far = swap(source, far_mask, n_times)
        early = {0: source} | {m: swap(source, m, n_times) for m in near}
        early[far_mask] = far
        far, product = lax.optimization_barrier((far, product))
        late = {far_mask ^ m: swap(far, m, n_times) for m in near}
        first = traces(product, back, early, nop, rows)
        result = traces(product, back, late, nop, rows, before=first, last=True)
    else:
        whole = lax.all_gather(source.reshape(2, nop, own_rows, order), "ta", axis=2, tiled=True)
        pieces = {
            k: whole[:, :, k * rows : (k + 1) * rows].reshape(-1, order) for k in range(order // rows)
        }
        result = traces(product, back, pieces, nop, rows, known=True, last=True)
    return result[:, None]


def solution(mesh):
    placed = (
        P(("cfg", "ta"), "sa", None, None, None),
        P(("cfg", "sa"), "ta", None, None, None),
        P(("cfg", "ta"), None, "sa", None, None),
        P(("cfg", "sa"), None, "ta", None, None),
        P(),
        P(),
    )
    return jax.shard_map(
        functools.partial(per_device, n_times=mesh.shape["ta"]),
        mesh=mesh,
        in_specs=placed,
        out_specs=P(("cfg", "ta"), "sa", None, None, None),
        check_vma=False,
    )
```

```python
import functools

import jax
import jax.numpy as jnp
from jax import lax
from jax.experimental import pallas as pl
from jax.experimental.pallas import tpu as pltpu
from jax.sharding import PartitionSpec as P

NDISP = 3
VMEM_LIMIT = 40 * 1024 * 1024
WHOLE = pl.BlockSpec(memory_space=pltpu.VMEM)
IN_HBM = pl.BlockSpec(memory_space=pltpu.HBM)
IN_SMEM = pl.BlockSpec(memory_space=pltpu.SMEM)


def source_kernel(mom_ref, disp_ref, bank_ref, out_ref, entry_ref, mom, disp, bank, arrived):
    copies = [
        pltpu.make_async_copy(mom_ref, mom, arrived.at[0]),
        pltpu.make_async_copy(disp_ref, disp, arrived.at[1]),
        pltpu.make_async_copy(bank_ref, bank, arrived.at[2]),
    ]
    for copy in copies:
        copy.start()
    for copy in copies:
        copy.wait()
    for a in range(out_ref.shape[1]):
        entry_ref[a] = mom[a] * NDISP + disp[a]
        out_ref[:, a] = bank[:, entry_ref[a]]


def chosen_source_rows(bank, op_mom, op_disp):
    nop = op_mom.shape[0]
    return pl.pallas_call(
        source_kernel,
        out_shape=[
            pltpu.VMEM((bank.shape[0], nop) + bank.shape[2:], bank.dtype),
            pltpu.SMEM((nop,), jnp.int32),
        ],
        in_specs=[IN_HBM] * 3,
        out_specs=[WHOLE, IN_SMEM],
        scratch_shapes=[
            pltpu.SMEM((nop,), jnp.int32),
            pltpu.SMEM((nop,), jnp.int32),
            pltpu.VMEM(bank.shape, bank.dtype),
            pltpu.SemaphoreType.DMA((3,)),
        ],
        compiler_params=pltpu.CompilerParams(vmem_limit_bytes=VMEM_LIMIT),
        name="source_rows",
    )(*(pltpu.with_memory_space_constraint(x, pltpu.HBM) for x in (op_mom, op_disp, bank)))


def planar(matrices):
    return jnp.swapaxes(matrices, 1, 2)


def swap(array, mask, count):
    return lax.ppermute(array, "ta", [(k, k ^ mask) for k in range(count)])


def sink_kernel(entry_ref, forward_ref, own_ref, other_ref, out_ref, forward, rows, arrived):
    times, nop = rows.shape[:2]
    entries = [entry_ref[a] for a in range(nop)]
    whole = pltpu.make_async_copy(forward_ref, forward, arrived.at[nop])
    whole.start()
    copies = [
        pltpu.make_async_copy(own_ref.at[:, e], rows.at[:, a], arrived.at[a]) for a, e in enumerate(entries)
    ]
    for copy in copies:
        copy.start()
    mine = lax.axis_index("sa")

    def joined(matrices):
        split = [jnp.swapaxes(x, 0, 1) for x in matrices]
        return jnp.concatenate([jnp.concatenate([x[0], x[1]], axis=1) for x in split], axis=0)

    def multiply(half, lefts, rights):
        for t in range(times):
            out_ref[t, half] = lax.dot_general(
                lefts[t], rights[t], (((0,), (1,)), ((), ())), preferred_element_type=jnp.float32
            ).astype(jnp.bfloat16)

    rights = [joined([other_ref[t, e] for e in entries]) for t in range(times)]
    whole.wait()
    lefts = []
    for t in range(times):
        parts = jnp.swapaxes(forward[t, 0], 0, 1)
        for_real = jnp.concatenate([parts[0], -parts[1]], axis=0)
        for_imag = jnp.concatenate([parts[1], parts[0]], axis=0)
        lefts.append(jnp.concatenate([for_real, for_imag], axis=1))
    multiply(1 - mine, lefts, rights)
    for copy in copies:
        copy.wait()
    multiply(mine, lefts, [joined([rows[t, a] for a in range(nop)]) for t in range(times)])


def sink_products(forward, own_bank, other_bank, entries):
    nop = entries.shape[0]
    times, order = forward.shape[0], forward.shape[2]
    return pl.pallas_call(
        sink_kernel,
        out_shape=jax.ShapeDtypeStruct((times, 2, 2 * order, nop * own_bank.shape[2]), jnp.bfloat16),
        in_specs=[IN_SMEM, IN_HBM, IN_HBM, WHOLE],
        out_specs=WHOLE,
        scratch_shapes=[
            pltpu.VMEM(forward.shape, forward.dtype),
            pltpu.VMEM((times, nop) + own_bank.shape[2:], own_bank.dtype),
            pltpu.SemaphoreType.DMA((nop + 1,)),
        ],
        compiler_params=pltpu.CompilerParams(vmem_limit_bytes=VMEM_LIMIT),
        cost_estimate=pl.CostEstimate(
            flops=2 * times * 2 * order * 2 * order * order * nop,
            bytes_accessed=5 * 1024 * 1024,
            transcendentals=0,
        ),
        name="sink_product",
    )(
        pltpu.with_memory_space_constraint(entries, pltpu.SMEM),
        pltpu.with_memory_space_constraint(forward, pltpu.HBM),
        pltpu.with_memory_space_constraint(own_bank, pltpu.HBM),
        other_bank,
    )


def trace_kernel(masks, known, last, nop, rows, *refs):
    product_ref, back_ref = refs[:2]
    me = 0 if known else lax.axis_index("ta")
    piece_refs = refs[2 : 2 + len(masks)]
    before_ref = refs[2 + len(masks)] if len(refs) == 4 + len(masks) else None
    out_ref = refs[-1]
    times = product_ref.shape[0]
    order = back_ref.shape[2]
    totals = [None if before_ref is None else before_ref[t] for t in range(times)]
    for mask, piece_ref in zip(masks, piece_refs):
        height = piece_ref.shape[0] // 2
        real, imag = piece_ref[:height], piece_ref[height:]
        for_real = jnp.concatenate([real, -imag], axis=1)
        for_imag = jnp.concatenate([imag, real], axis=1)
        left = jnp.concatenate([for_real, for_imag], axis=0)
        start = pl.multiple_of((me ^ mask) * rows, rows)
        for t in range(times):
            reverse = jnp.dot(left, back_ref[t], preferred_element_type=jnp.float32)
            high = reverse.astype(jnp.bfloat16)
            low = (reverse - high.astype(jnp.float32)).astype(jnp.bfloat16)
            blocks = []
            for part in range(2):
                two = [
                    product_ref[t, half, pl.ds(part * order + start, rows), :]
                    for half in range(2)
                ]
                width = two[0].shape[1] // nop
                for a in range(nop):
                    blocks.append(
                        jnp.concatenate([x[:, a * width : (a + 1) * width] for x in two], axis=1)
                    )
            sink = jnp.concatenate(blocks, axis=0)
            nt = (((1,), (1,)), ((), ()))
            added = lax.dot_general(sink, high, nt, preferred_element_type=jnp.float32)
            added += lax.dot_general(sink, low, nt, preferred_element_type=jnp.float32)
            totals[t] = added if totals[t] is None else totals[t] + added
    if not last:
        for t in range(times):
            out_ref[t] = totals[t]
        return
    width = nop * rows
    same = lax.broadcasted_iota(jnp.int32, (rows, width), 0) == lax.rem(
        lax.broadcasted_iota(jnp.int32, (rows, width), 1), rows
    )
    sums = []
    for t in range(times):
        kept = [
            jnp.where(same, totals[t][:, d * width : (d + 1) * width].reshape(2, nop, rows, width), 0.0)
            for d in range(2)
        ]
        sums.append(kept[0][0] - kept[1][1])
        sums.append(kept[1][0] + kept[0][1])
    left_over = jnp.concatenate(sums, axis=0).sum(axis=1)
    height = left_over.shape[0]
    terms = []
    for _ in range(3):
        terms.append(left_over.astype(jnp.bfloat16))
        left_over = left_over - terms[-1].astype(jnp.float32)
    of_operator = (
        lax.broadcasted_iota(jnp.int32, (width, nop), 0) // rows
        == lax.broadcasted_iota(jnp.int32, (width, nop), 1)
    ).astype(jnp.bfloat16)
    paired = jnp.dot(jnp.concatenate(terms, axis=0), of_operator, preferred_element_type=jnp.float32)
    paired = (paired[:height] + (paired[height : 2 * height] + paired[2 * height :])) / order
    for t in range(times):
        for part in range(2):
            at = (2 * t + part) * nop
            out_ref[t, part] = paired[at : at + nop]


def traces(product, back, pieces, nop, rows, known=False, before=None, last=False):
    times, order = product.shape[0], back.shape[2]
    side = 2 * nop * rows
    operands = [product, back, *pieces.values()] + ([] if before is None else [before])
    shape = (times, 2, nop, nop) if last else (times, side, side)
    flops = 2 * times * len(pieces) * side * (2 * order * order + 2 * side * order)
    return pl.pallas_call(
        functools.partial(trace_kernel, tuple(pieces), known, last, nop, rows),
        out_shape=jax.ShapeDtypeStruct(shape, jnp.float32),
        in_specs=[WHOLE] * len(operands),
        out_specs=WHOLE,
        compiler_params=pltpu.CompilerParams(vmem_limit_bytes=VMEM_LIMIT),
        cost_estimate=pl.CostEstimate(flops=flops, bytes_accessed=4 * 1024 * 1024, transcendentals=0),
        name="traces_last" if last else "traces",
    )(*operands)


def per_device(forward, backward, sink_bank, source_bank, op_mom, op_disp, n_times):
    nop = op_mom.shape[0]
    order = forward.shape[2]
    times = forward.shape[0]
    own_rows = source_bank.shape[2]

    source_raw, entries = chosen_source_rows(source_bank, op_mom, op_disp)
    source = jnp.transpose(source_raw[0], (2, 0, 1, 3)).reshape(-1, order)
    other_bank = lax.ppermute(sink_bank, "sa", [(0, 1), (1, 0)])
    product = sink_products(
        forward,
        sink_bank,
        other_bank,
        entries,
    )
    back = planar(backward[0]).reshape(times, 2 * order, order)

    rows = order // (2 * nop)
    far_mask = n_times // 2
    if own_rows == rows and n_times == 2 * far_mask and far_mask & (far_mask - 1) == 0:
        near = range(1, far_mask)
        far = swap(source, far_mask, n_times)
        early = {0: source} | {m: swap(source, m, n_times) for m in reversed(near)}
        early[far_mask] = far
        far, product = lax.optimization_barrier((far, product))
        late = {far_mask ^ m: swap(far, m, n_times) for m in near}
        first = traces(product, back, early, nop, rows)
        end = {far_mask ^ near[-1]: late.pop(far_mask ^ near[-1])}
        first = traces(product, back, late, nop, rows, before=first)
        result = traces(product, back, end, nop, rows, before=first, last=True)
    else:
        whole = lax.all_gather(source.reshape(2, nop, own_rows, order), "ta", axis=2, tiled=True)
        pieces = {
            k: whole[:, :, k * rows : (k + 1) * rows].reshape(-1, order) for k in range(order // rows)
        }
        result = traces(product, back, pieces, nop, rows, known=True, last=True)
    return result[:, None]


def solution(mesh):
    placed = (
        P(("cfg", "ta"), "sa", None, None, None),
        P(("cfg", "sa"), "ta", None, None, None),
        P(("cfg", "ta"), None, "sa", None, None),
        P(("cfg", "sa"), None, "ta", None, None),
        P(),
        P(),
    )
    return jax.shard_map(
        functools.partial(per_device, n_times=mesh.shape["ta"]),
        mesh=mesh,
        in_specs=placed,
        out_specs=P(("cfg", "ta"), "sa", None, None, None),
        check_vma=False,
    )
```

```python
import functools

import jax
import jax.numpy as jnp
from jax import lax
from jax.experimental import pallas as pl
from jax.experimental.pallas import tpu as pltpu
from jax.sharding import PartitionSpec as P

NDISP = 3
VMEM_LIMIT = 40 * 1024 * 1024
WHOLE = pl.BlockSpec(memory_space=pltpu.VMEM)
IN_HBM = pl.BlockSpec(memory_space=pltpu.HBM)
IN_SMEM = pl.BlockSpec(memory_space=pltpu.SMEM)


def source_kernel(mom_ref, disp_ref, bank_ref, out_ref, entry_ref, mom, disp, bank, arrived):
    copies = [
        pltpu.make_async_copy(mom_ref, mom, arrived.at[0]),
        pltpu.make_async_copy(disp_ref, disp, arrived.at[1]),
        pltpu.make_async_copy(bank_ref, bank, arrived.at[2]),
    ]
    for copy in copies:
        copy.start()
    for copy in copies:
        copy.wait()
    for a in range(out_ref.shape[0]):
        entry = mom[a] * NDISP + disp[a]
        entry_ref[a] = entry
        out_ref[a] = jnp.swapaxes(bank[0, entry], 0, 1)


def chosen_source_rows(bank, op_mom, op_disp):
    nop = op_mom.shape[0]
    return pl.pallas_call(
        source_kernel,
        out_shape=[
            pltpu.VMEM((nop, bank.shape[3], bank.shape[2], bank.shape[4]), bank.dtype),
            pltpu.SMEM((nop,), jnp.int32),
        ],
        in_specs=[IN_HBM] * 3,
        out_specs=[WHOLE, IN_SMEM],
        scratch_shapes=[
            pltpu.SMEM((nop,), jnp.int32),
            pltpu.SMEM((nop,), jnp.int32),
            pltpu.VMEM(bank.shape, bank.dtype),
            pltpu.SemaphoreType.DMA((3,)),
        ],
        compiler_params=pltpu.CompilerParams(vmem_limit_bytes=VMEM_LIMIT),
        name="source_rows",
    )(*(pltpu.with_memory_space_constraint(x, pltpu.HBM) for x in (op_mom, op_disp, bank)))


def planar(matrices):
    return jnp.swapaxes(matrices, 1, 2)


def swap(array, masks, count):
    cores = len(masks)
    pairs = [(k * cores + c, (k ^ m) * cores + c) for k in range(count) for c, m in enumerate(masks)]
    return lax.ppermute(array, ("ta", "sa"), pairs)


def sink_kernel(entry_ref, forward_ref, own_ref, other_ref, out_ref, forward, rows, arrived):
    times, nop = rows.shape[:2]
    entries = [entry_ref[a] for a in range(nop)]
    whole = pltpu.make_async_copy(forward_ref, forward, arrived.at[nop])
    whole.start()
    copies = [
        pltpu.make_async_copy(own_ref.at[:, e], rows.at[:, a], arrived.at[a]) for a, e in enumerate(entries)
    ]
    for copy in copies:
        copy.start()
    mine = lax.axis_index("sa")

    def joined(matrices):
        split = [jnp.swapaxes(x, 0, 1) for x in matrices]
        return jnp.concatenate([jnp.concatenate([x[0], x[1]], axis=1) for x in split], axis=0)

    def multiply(half, lefts, rights):
        for t in range(times):
            out_ref[t, half] = lax.dot_general(
                lefts[t], rights[t], (((0,), (1,)), ((), ())), preferred_element_type=jnp.float32
            ).astype(jnp.bfloat16)

    rights = [joined([other_ref[t, e] for e in entries]) for t in range(times)]
    whole.wait()
    lefts = []
    for t in range(times):
        parts = jnp.swapaxes(forward[t, 0], 0, 1)
        for_real = jnp.concatenate([parts[0], -parts[1]], axis=0)
        for_imag = jnp.concatenate([parts[1], parts[0]], axis=0)
        lefts.append(jnp.concatenate([for_real, for_imag], axis=1))
    multiply(1 - mine, lefts, rights)
    for copy in copies:
        copy.wait()
    multiply(mine, lefts, [joined([rows[t, a] for a in range(nop)]) for t in range(times)])


def sink_products(forward, own_bank, other_bank, entries):
    nop = entries.shape[0]
    times, order = forward.shape[0], forward.shape[2]
    return pl.pallas_call(
        sink_kernel,
        out_shape=jax.ShapeDtypeStruct((times, 2, 2 * order, nop * own_bank.shape[2]), jnp.bfloat16),
        in_specs=[IN_SMEM, IN_HBM, IN_HBM, WHOLE],
        out_specs=WHOLE,
        scratch_shapes=[
            pltpu.VMEM(forward.shape, forward.dtype),
            pltpu.VMEM((times, nop) + own_bank.shape[2:], own_bank.dtype),
            pltpu.SemaphoreType.DMA((nop + 1,)),
        ],
        compiler_params=pltpu.CompilerParams(vmem_limit_bytes=VMEM_LIMIT),
        cost_estimate=pl.CostEstimate(
            flops=2 * times * 2 * order * 2 * order * order * nop,
            bytes_accessed=5 * 1024 * 1024,
            transcendentals=0,
        ),
        name="sink_product",
    )(
        pltpu.with_memory_space_constraint(entries, pltpu.SMEM),
        pltpu.with_memory_space_constraint(forward, pltpu.HBM),
        pltpu.with_memory_space_constraint(own_bank, pltpu.HBM),
        other_bank,
    )


def own_mask(masks, core):
    mask = masks[0]
    for c, m in enumerate(masks[1:], 1):
        mask = jnp.where(core == c, m, mask) if m != masks[0] else mask
    return mask


def sink_block(product_ref, t, start, nop, rows):
    order = product_ref.shape[2] // 2
    width = product_ref.shape[3] // nop
    parts = []
    for part in range(2):
        two = [product_ref[t, half, pl.ds(part * order + start, rows), :] for half in range(2)]
        parts.append(
            jnp.concatenate(
                [
                    jnp.concatenate([x[:, a * width : (a + 1) * width] for x in two], axis=1)
                    for a in range(nop)
                ],
                axis=0,
            )
        )
    return parts


def block_start(masks, rows, known):
    if known:
        return masks[0] * rows
    return pl.multiple_of((lax.axis_index("ta") ^ own_mask(masks, lax.axis_index("sa"))) * rows, rows)


def diagonal_sums(tables, nop, rows):
    width = nop * rows
    same = lax.broadcasted_iota(jnp.int32, (rows, width), 0) == lax.rem(
        lax.broadcasted_iota(jnp.int32, (rows, width), 1), rows
    )
    return jnp.concatenate(
        [jnp.where(same, x.reshape(nop, rows, width), 0.0) for x in tables], axis=0
    ).sum(axis=1)


def trace_kernel(masks, known, sums, nop, rows, *refs):
    product_ref, back_ref = refs[:2]
    piece_refs = refs[2 : 2 + len(masks)]
    before_ref = refs[2 + len(masks)] if len(refs) == 4 + len(masks) else None
    out_ref = refs[-1]
    times = product_ref.shape[0]
    order = back_ref.shape[2]
    totals = [None if before_ref is None else before_ref[t] for t in range(times)]
    nt = (((1,), (1,)), ((), ()))
    for mask, piece_ref in zip(masks, piece_refs):
        real, imag = (piece_ref[:, part].reshape(nop * rows, order) for part in range(2))
        for_real = jnp.concatenate([real, -imag], axis=1)
        for_imag = jnp.concatenate([imag, real], axis=1)
        left = jnp.concatenate([for_real, for_imag], axis=0)
        start = block_start(mask, rows, known)
        for t in range(times):
            reverse = jnp.dot(left, back_ref[t], preferred_element_type=jnp.float32)
            high = reverse.astype(jnp.bfloat16)
            low = (reverse - high.astype(jnp.float32)).astype(jnp.bfloat16)
            sink = jnp.concatenate(sink_block(product_ref, t, start, nop, rows), axis=0)
            added = lax.dot_general(sink, high, nt, preferred_element_type=jnp.float32)
            added += lax.dot_general(sink, low, nt, preferred_element_type=jnp.float32)
            totals[t] = added if totals[t] is None else totals[t] + added
    if not sums:
        for t in range(times):
            out_ref[t] = totals[t]
        return
    width = nop * rows
    tables = []
    for total in totals:
        (rr, ri), (ir, ii) = (
            [total[c * width : (c + 1) * width, d * width : (d + 1) * width] for d in range(2)] for c in range(2)
        )
        tables += [rr - ii, ri + ir]
    out_ref[...] = diagonal_sums(tables, nop, rows)


def traces(product, back, pieces, nop, rows, known=False, before=None, sums=False):
    times, order = product.shape[0], back.shape[2]
    side = 2 * nop * rows
    operands = [product, back, *pieces.values()] + ([] if before is None else [before])
    shape = (times * 2 * nop, nop * rows) if sums else (times, side, side)
    flops = 2 * times * len(pieces) * side * (2 * order * order + 2 * side * order)
    return pl.pallas_call(
        functools.partial(trace_kernel, tuple(pieces), known, sums, nop, rows),
        out_shape=jax.ShapeDtypeStruct(shape, jnp.float32),
        in_specs=[WHOLE] * len(operands),
        out_specs=WHOLE,
        compiler_params=pltpu.CompilerParams(vmem_limit_bytes=VMEM_LIMIT),
        cost_estimate=pl.CostEstimate(flops=flops, bytes_accessed=4 * 1024 * 1024, transcendentals=0),
        name="trace_sums" if sums else "traces",
    )(*operands)


def loop_kernel(masks, nop, rows, product_ref, back_ref, after_ref, out_ref):
    order = back_ref.shape[2]
    start = block_start(masks, rows, False)
    for t in range(product_ref.shape[0]):
        back = jnp.concatenate([back_ref[t, :order], back_ref[t, order:]], axis=1)
        real, imag = sink_block(product_ref, t, start, nop, rows)
        value = [
            lax.dot_general(x, back, (((1,), (1,)), ((), ())), preferred_element_type=jnp.float32)
            for x in (jnp.concatenate([real, -imag], axis=1), jnp.concatenate([imag, real], axis=1))
        ]
        for term in range(2):
            now = [x.astype(jnp.bfloat16) for x in value]
            value = [x - y.astype(jnp.float32) for x, y in zip(value, now)]
            out_ref[t, term, 0] = jnp.concatenate([now[0], -now[1]], axis=1)
            out_ref[t, term, 1] = jnp.concatenate([now[1], now[0]], axis=1)


def last_kernel(nop, rows, order, *refs):
    left_over = refs[0][...]
    out_ref = refs[-1]
    times = out_ref.shape[0]
    width = nop * rows
    if len(refs) > 2:
        piece_ref, loop_ref = refs[1:3]
        piece = jnp.concatenate([piece_ref[:, part].reshape(width, order) for part in range(2)], axis=1)
        met = loop_ref[...].reshape(-1, 2 * order)
        found = lax.dot_general(met, piece, (((1,), (1,)), ((), ())), preferred_element_type=jnp.float32)
        found = found.reshape(times, 2, 2, width, width)
        tables = [found[t, 0, part] + found[t, 1, part] for t in range(times) for part in range(2)]
        left_over = left_over + diagonal_sums(tables, nop, rows)
    height = left_over.shape[0]
    terms = []
    for _ in range(3):
        terms.append(left_over.astype(jnp.bfloat16))
        left_over = left_over - terms[-1].astype(jnp.float32)
    of_operator = (
        lax.broadcasted_iota(jnp.int32, (width, nop), 0) // rows
        == lax.broadcasted_iota(jnp.int32, (width, nop), 1)
    ).astype(jnp.bfloat16)
    paired = jnp.dot(jnp.concatenate(terms, axis=0), of_operator, preferred_element_type=jnp.float32)
    paired = (paired[:height] + (paired[height : 2 * height] + paired[2 * height :])) / order
    for t in range(times):
        for part in range(2):
            at = (2 * t + part) * nop
            out_ref[t, part] = paired[at : at + nop]


def finish(sums, nop, rows, order, *more):
    return pl.pallas_call(
        functools.partial(last_kernel, nop, rows, order),
        out_shape=jax.ShapeDtypeStruct((sums.shape[0] // (2 * nop), 2, nop, nop), jnp.float32),
        in_specs=[WHOLE] * (1 + len(more)),
        out_specs=WHOLE,
        compiler_params=pltpu.CompilerParams(vmem_limit_bytes=VMEM_LIMIT),
        name="traces_last",
    )(sums, *more)


def loops(product, back, after, masks, nop, rows):
    times, order = product.shape[0], back.shape[2]
    return pl.pallas_call(
        functools.partial(loop_kernel, masks, nop, rows),
        out_shape=jax.ShapeDtypeStruct((times, 2, 2, nop * rows, 2 * order), jnp.bfloat16),
        in_specs=[WHOLE, WHOLE, pl.BlockSpec(memory_space=pl.ANY)],
        out_specs=WHOLE,
        compiler_params=pltpu.CompilerParams(vmem_limit_bytes=VMEM_LIMIT),
        name="loops",
    )(product, back, after)


def per_device(forward, backward, sink_bank, source_bank, op_mom, op_disp, n_times):
    nop = op_mom.shape[0]
    order = forward.shape[2]
    times = forward.shape[0]
    own_rows = source_bank.shape[2]

    source, entries = chosen_source_rows(source_bank, op_mom, op_disp)
    other_bank = lax.ppermute(sink_bank, "sa", [(0, 1), (1, 0)])
    product = sink_products(
        forward,
        sink_bank,
        other_bank,
        entries,
    )
    back = planar(backward[0]).reshape(times, 2 * order, order)

    rows = order // (2 * nop)
    far_mask = n_times // 2
    if own_rows == rows and n_times == 2 * far_mask and far_mask & (far_mask - 1) == 0:
        near = tuple(range(1, far_mask))
        orders = (near[::-1], (near[1:-1] + near[:1] + near[-1:]))
        far = swap(source, (far_mask, far_mask), n_times)
        early = {(0, 0): source} | {m: swap(source, m, n_times) for m in zip(*orders)}
        early[far_mask, far_mask] = far
        far, product = lax.optimization_barrier((far, product))
        late = {(far_mask ^ m[0], far_mask ^ m[1]): swap(far, m, n_times) for m in zip(near, near)}
        first = traces(product, back, early, nop, rows)
        last_masks = list(late)[-1]
        end = late.pop(last_masks)
        loop = loops(product, back, first, last_masks, nop, rows)
        sums = traces(product, back, late, nop, rows, before=first, sums=True)
        result = finish(sums, nop, rows, order, end, loop)
    else:
        whole = lax.all_gather(source, "ta", axis=2, tiled=True)
        pieces = {(k,): whole[:, :, k * rows : (k + 1) * rows] for k in range(order // rows)}
        sums = traces(product, back, pieces, nop, rows, known=True, sums=True)
        result = finish(sums, nop, rows, order)
    return result[:, None]


def solution(mesh):
    placed = (
        P(("cfg", "ta"), "sa", None, None, None),
        P(("cfg", "sa"), "ta", None, None, None),
        P(("cfg", "ta"), None, "sa", None, None),
        P(("cfg", "sa"), None, "ta", None, None),
        P(),
        P(),
    )
    return jax.shard_map(
        functools.partial(per_device, n_times=mesh.shape["ta"]),
        mesh=mesh,
        in_specs=placed,
        out_specs=P(("cfg", "ta"), "sa", None, None, None),
        check_vma=False,
    )
```

```python
import functools

import jax
import jax.numpy as jnp
from jax import lax
from jax.experimental import pallas as pl
from jax.experimental.pallas import tpu as pltpu
from jax.sharding import PartitionSpec as P

NDISP = 3
VMEM_LIMIT = 40 * 1024 * 1024
WHOLE = pl.BlockSpec(memory_space=pltpu.VMEM)
IN_HBM = pl.BlockSpec(memory_space=pltpu.HBM)
IN_SMEM = pl.BlockSpec(memory_space=pltpu.SMEM)


def source_kernel(mom_ref, disp_ref, bank_ref, out_ref, entry_ref, mom, disp, bank, arrived):
    copies = [
        pltpu.make_async_copy(mom_ref, mom, arrived.at[0]),
        pltpu.make_async_copy(disp_ref, disp, arrived.at[1]),
        pltpu.make_async_copy(bank_ref, bank, arrived.at[2]),
    ]
    for copy in copies:
        copy.start()
    for copy in copies:
        copy.wait()
    for a in range(out_ref.shape[0]):
        entry = mom[a] * NDISP + disp[a]
        entry_ref[a] = entry
        out_ref[a] = jnp.swapaxes(bank[0, entry], 0, 1)


def chosen_source_rows(bank, op_mom, op_disp):
    nop = op_mom.shape[0]
    return pl.pallas_call(
        source_kernel,
        out_shape=[
            pltpu.VMEM((nop, bank.shape[3], bank.shape[2], bank.shape[4]), bank.dtype),
            pltpu.SMEM((nop,), jnp.int32),
        ],
        in_specs=[IN_HBM] * 3,
        out_specs=[WHOLE, IN_SMEM],
        scratch_shapes=[
            pltpu.SMEM((nop,), jnp.int32),
            pltpu.SMEM((nop,), jnp.int32),
            pltpu.VMEM(bank.shape, bank.dtype),
            pltpu.SemaphoreType.DMA((3,)),
        ],
        compiler_params=pltpu.CompilerParams(vmem_limit_bytes=VMEM_LIMIT),
        name="source_rows",
    )(*(pltpu.with_memory_space_constraint(x, pltpu.HBM) for x in (op_mom, op_disp, bank)))


def planar(matrices):
    return jnp.swapaxes(matrices, 1, 2)


def swap(array, masks, count):
    cores = len(masks)
    pairs = [(k * cores + c, (k ^ m) * cores + c) for k in range(count) for c, m in enumerate(masks)]
    return lax.ppermute(array, ("ta", "sa"), pairs)


def sink_kernel(entry_ref, forward_ref, own_ref, other_ref, out_ref, forward, rows, arrived):
    times, nop = rows.shape[:2]
    entries = [entry_ref[a] for a in range(nop)]
    whole = pltpu.make_async_copy(forward_ref, forward, arrived.at[nop])
    whole.start()
    copies = [
        pltpu.make_async_copy(own_ref.at[:, e], rows.at[:, a], arrived.at[a]) for a, e in enumerate(entries)
    ]
    for copy in copies:
        copy.start()
    mine = lax.axis_index("sa")

    def joined(matrices):
        split = [jnp.swapaxes(x, 0, 1) for x in matrices]
        return jnp.concatenate([jnp.concatenate([x[0], x[1]], axis=1) for x in split], axis=0)

    def multiply(half, lefts, rights):
        for t in range(times):
            out_ref[t, half] = lax.dot_general(
                lefts[t], rights[t], (((0,), (1,)), ((), ())), preferred_element_type=jnp.float32
            ).astype(jnp.bfloat16)

    rights = [joined([other_ref[t, e] for e in entries]) for t in range(times)]
    whole.wait()
    lefts = []
    for t in range(times):
        parts = jnp.swapaxes(forward[t, 0], 0, 1)
        for_real = jnp.concatenate([parts[0], -parts[1]], axis=0)
        for_imag = jnp.concatenate([parts[1], parts[0]], axis=0)
        lefts.append(jnp.concatenate([for_real, for_imag], axis=1))
    multiply(1 - mine, lefts, rights)
    for copy in copies:
        copy.wait()
    multiply(mine, lefts, [joined([rows[t, a] for a in range(nop)]) for t in range(times)])


def sink_products(forward, own_bank, other_bank, entries):
    nop = entries.shape[0]
    times, order = forward.shape[0], forward.shape[2]
    return pl.pallas_call(
        sink_kernel,
        out_shape=jax.ShapeDtypeStruct((times, 2, 2 * order, nop * own_bank.shape[2]), jnp.bfloat16),
        in_specs=[IN_SMEM, IN_HBM, IN_HBM, WHOLE],
        out_specs=WHOLE,
        scratch_shapes=[
            pltpu.VMEM(forward.shape, forward.dtype),
            pltpu.VMEM((times, nop) + own_bank.shape[2:], own_bank.dtype),
            pltpu.SemaphoreType.DMA((nop + 1,)),
        ],
        compiler_params=pltpu.CompilerParams(vmem_limit_bytes=VMEM_LIMIT),
        cost_estimate=pl.CostEstimate(
            flops=2 * times * 2 * order * 2 * order * order * nop,
            bytes_accessed=5 * 1024 * 1024,
            transcendentals=0,
        ),
        name="sink_product",
    )(
        pltpu.with_memory_space_constraint(entries, pltpu.SMEM),
        pltpu.with_memory_space_constraint(forward, pltpu.HBM),
        pltpu.with_memory_space_constraint(own_bank, pltpu.HBM),
        other_bank,
    )


def own_mask(masks, core):
    mask = masks[0]
    for c, m in enumerate(masks[1:], 1):
        mask = jnp.where(core == c, m, mask) if m != masks[0] else mask
    return mask


def sink_block(product_ref, t, start, nop, rows):
    order = product_ref.shape[2] // 2
    width = product_ref.shape[3] // nop
    parts = []
    for part in range(2):
        two = [product_ref[t, half, pl.ds(part * order + start, rows), :] for half in range(2)]
        parts.append(
            jnp.concatenate(
                [
                    jnp.concatenate([x[:, a * width : (a + 1) * width] for x in two], axis=1)
                    for a in range(nop)
                ],
                axis=0,
            )
        )
    return parts


def block_start(masks, rows, known):
    if known:
        return masks[0] * rows
    return pl.multiple_of((lax.axis_index("ta") ^ own_mask(masks, lax.axis_index("sa"))) * rows, rows)


def diagonal_sums(tables, nop, rows):
    width = nop * rows
    same = lax.broadcasted_iota(jnp.int32, (rows, width), 0) == lax.rem(
        lax.broadcasted_iota(jnp.int32, (rows, width), 1), rows
    )
    return jnp.concatenate(
        [jnp.where(same, x.reshape(nop, rows, width), 0.0) for x in tables], axis=0
    ).sum(axis=1)


def trace_kernel(masks, known, sums, nop, rows, *refs):
    product_ref, back_ref = refs[:2]
    piece_refs = refs[2 : 2 + len(masks)]
    before_ref = refs[2 + len(masks)] if len(refs) == 4 + len(masks) else None
    out_ref = refs[-1]
    times = product_ref.shape[0]
    order = back_ref.shape[2]
    totals = [None if before_ref is None else before_ref[t] for t in range(times)]
    nt = (((1,), (1,)), ((), ()))
    for mask, piece_ref in zip(masks, piece_refs):
        real, imag = (piece_ref[:, part].reshape(nop * rows, order) for part in range(2))
        for_real = jnp.concatenate([real, -imag], axis=1)
        for_imag = jnp.concatenate([imag, real], axis=1)
        left = jnp.concatenate([for_real, for_imag], axis=0)
        start = block_start(mask, rows, known)
        for t in range(times):
            reverse = jnp.dot(left, back_ref[t], preferred_element_type=jnp.float32)
            high = reverse.astype(jnp.bfloat16)
            low = (reverse - high.astype(jnp.float32)).astype(jnp.bfloat16)
            sink = jnp.concatenate(sink_block(product_ref, t, start, nop, rows), axis=0)
            added = lax.dot_general(sink, high, nt, preferred_element_type=jnp.float32)
            added += lax.dot_general(sink, low, nt, preferred_element_type=jnp.float32)
            totals[t] = added if totals[t] is None else totals[t] + added
    if not sums:
        for t in range(times):
            out_ref[t] = totals[t]
        return
    width = nop * rows
    tables = []
    for total in totals:
        (rr, ri), (ir, ii) = (
            [total[c * width : (c + 1) * width, d * width : (d + 1) * width] for d in range(2)] for c in range(2)
        )
        tables += [rr - ii, ri + ir]
    out_ref[...] = diagonal_sums(tables, nop, rows)


def traces(product, back, pieces, nop, rows, known=False, before=None, sums=False):
    times, order = product.shape[0], back.shape[2]
    side = 2 * nop * rows
    operands = [product, back, *pieces.values()] + ([] if before is None else [before])
    shape = (times * 2 * nop, nop * rows) if sums else (times, side, side)
    flops = 2 * times * len(pieces) * side * (2 * order * order + 2 * side * order)
    return pl.pallas_call(
        functools.partial(trace_kernel, tuple(pieces), known, sums, nop, rows),
        out_shape=jax.ShapeDtypeStruct(shape, jnp.float32),
        in_specs=[WHOLE] * len(operands),
        out_specs=WHOLE,
        compiler_params=pltpu.CompilerParams(vmem_limit_bytes=VMEM_LIMIT),
        cost_estimate=pl.CostEstimate(flops=flops, bytes_accessed=4 * 1024 * 1024, transcendentals=0),
        name="trace_sums" if sums else "traces",
    )(*operands)


def loop_kernel(masks, nop, rows, product_ref, back_ref, after_ref, out_ref):
    order = back_ref.shape[2]
    start = block_start(masks, rows, False)
    for t in range(product_ref.shape[0]):
        back = jnp.concatenate([back_ref[t, :order], back_ref[t, order:]], axis=1)
        real, imag = sink_block(product_ref, t, start, nop, rows)
        value = [
            lax.dot_general(x, back, (((1,), (1,)), ((), ())), preferred_element_type=jnp.float32)
            for x in (jnp.concatenate([real, -imag], axis=1), jnp.concatenate([imag, real], axis=1))
        ]
        for term in range(2):
            now = [x.astype(jnp.bfloat16) for x in value]
            value = [x - y.astype(jnp.float32) for x, y in zip(value, now)]
            at = slice(term * 2 * order, (term + 1) * 2 * order)
            out_ref[t, 0, :, at] = jnp.concatenate([now[0], -now[1]], axis=1)
            out_ref[t, 1, :, at] = jnp.concatenate([now[1], now[0]], axis=1)


def last_kernel(nop, rows, order, *refs):
    left_over = refs[0][...]
    out_ref = refs[-1]
    times = out_ref.shape[0]
    width = nop * rows
    if len(refs) > 2:
        piece_ref, loop_ref = refs[1:3]
        piece = jnp.concatenate([piece_ref[:, part].reshape(width, order) for part in range(2)], axis=1)
        met = loop_ref[...].reshape(-1, 4 * order)
        twice = jnp.concatenate([piece, piece], axis=1)
        found = lax.dot_general(met, twice, (((1,), (1,)), ((), ())), preferred_element_type=jnp.float32)
        found = found.reshape(times, 2, width, width)
        tables = [found[t, part] for t in range(times) for part in range(2)]
        left_over = left_over + diagonal_sums(tables, nop, rows)
    height = left_over.shape[0]
    terms = []
    for _ in range(3):
        terms.append(left_over.astype(jnp.bfloat16))
        left_over = left_over - terms[-1].astype(jnp.float32)
    of_operator = (
        lax.broadcasted_iota(jnp.int32, (width, nop), 0) // rows
        == lax.broadcasted_iota(jnp.int32, (width, nop), 1)
    ).astype(jnp.bfloat16)
    paired = jnp.dot(jnp.concatenate(terms, axis=0), of_operator, preferred_element_type=jnp.float32)
    paired = (paired[:height] + (paired[height : 2 * height] + paired[2 * height :])) / order
    for t in range(times):
        for part in range(2):
            at = (2 * t + part) * nop
            out_ref[t, part] = paired[at : at + nop]


def finish(sums, nop, rows, order, *more):
    return pl.pallas_call(
        functools.partial(last_kernel, nop, rows, order),
        out_shape=jax.ShapeDtypeStruct((sums.shape[0] // (2 * nop), 2, nop, nop), jnp.float32),
        in_specs=[WHOLE] * (1 + len(more)),
        out_specs=WHOLE,
        compiler_params=pltpu.CompilerParams(vmem_limit_bytes=VMEM_LIMIT),
        name="traces_last",
    )(sums, *more)


def loops(product, back, after, masks, nop, rows):
    times, order = product.shape[0], back.shape[2]
    return pl.pallas_call(
        functools.partial(loop_kernel, masks, nop, rows),
        out_shape=jax.ShapeDtypeStruct((times, 2, nop * rows, 4 * order), jnp.bfloat16),
        in_specs=[WHOLE, WHOLE, pl.BlockSpec(memory_space=pl.ANY)],
        out_specs=WHOLE,
        compiler_params=pltpu.CompilerParams(vmem_limit_bytes=VMEM_LIMIT),
        name="loops",
    )(product, back, after)


def per_device(forward, backward, sink_bank, source_bank, op_mom, op_disp, n_times):
    nop = op_mom.shape[0]
    order = forward.shape[2]
    times = forward.shape[0]
    own_rows = source_bank.shape[2]

    source, entries = chosen_source_rows(source_bank, op_mom, op_disp)
    other_bank = lax.ppermute(sink_bank, "sa", [(0, 1), (1, 0)])
    product = sink_products(
        forward,
        sink_bank,
        other_bank,
        entries,
    )
    back = planar(backward[0]).reshape(times, 2 * order, order)

    rows = order // (2 * nop)
    far_mask = n_times // 2
    if own_rows == rows and n_times == 2 * far_mask and far_mask & (far_mask - 1) == 0:
        near = tuple(range(1, far_mask))
        orders = (near[::-1], (near[1:-1] + near[:1] + near[-1:]))
        far = swap(source, (far_mask, far_mask), n_times)
        early = {(0, 0): source} | {m: swap(source, m, n_times) for m in zip(*orders)}
        early[far_mask, far_mask] = far
        far, product = lax.optimization_barrier((far, product))
        late = {(far_mask ^ m[0], far_mask ^ m[1]): swap(far, m, n_times) for m in zip(near, near)}
        first = traces(product, back, early, nop, rows)
        last_masks = list(late)[-1]
        end = late.pop(last_masks)
        loop = loops(product, back, first, last_masks, nop, rows)
        sums = traces(product, back, late, nop, rows, before=first, sums=True)
        result = finish(sums, nop, rows, order, end, loop)
    else:
        whole = lax.all_gather(source, "ta", axis=2, tiled=True)
        pieces = {(k,): whole[:, :, k * rows : (k + 1) * rows] for k in range(order // rows)}
        sums = traces(product, back, pieces, nop, rows, known=True, sums=True)
        result = finish(sums, nop, rows, order)
    return result[:, None]


def solution(mesh):
    placed = (
        P(("cfg", "ta"), "sa", None, None, None),
        P(("cfg", "sa"), "ta", None, None, None),
        P(("cfg", "ta"), None, "sa", None, None),
        P(("cfg", "sa"), None, "ta", None, None),
        P(),
        P(),
    )
    return jax.shard_map(
        functools.partial(per_device, n_times=mesh.shape["ta"]),
        mesh=mesh,
        in_specs=placed,
        out_specs=P(("cfg", "ta"), "sa", None, None, None),
        check_vma=False,
    )
```

```python
import functools

import jax
import jax.numpy as jnp
from jax import lax
from jax.experimental import pallas as pl
from jax.experimental.pallas import tpu as pltpu
from jax.sharding import PartitionSpec as P

NDISP = 3
VMEM_LIMIT = 40 * 1024 * 1024
WHOLE = pl.BlockSpec(memory_space=pltpu.VMEM)
IN_HBM = pl.BlockSpec(memory_space=pltpu.HBM)
IN_SMEM = pl.BlockSpec(memory_space=pltpu.SMEM)


def source_kernel(mom_ref, disp_ref, bank_ref, out_ref, entry_ref, mom, disp, bank, arrived):
    copies = [
        pltpu.make_async_copy(mom_ref, mom, arrived.at[0]),
        pltpu.make_async_copy(disp_ref, disp, arrived.at[1]),
        pltpu.make_async_copy(bank_ref, bank, arrived.at[2]),
    ]
    for copy in copies:
        copy.start()
    for copy in copies:
        copy.wait()
    for a in range(out_ref.shape[0]):
        entry = mom[a] * NDISP + disp[a]
        entry_ref[a] = entry
        out_ref[a] = jnp.swapaxes(bank[0, entry], 0, 1)


def chosen_source_rows(bank, op_mom, op_disp):
    nop = op_mom.shape[0]
    return pl.pallas_call(
        source_kernel,
        out_shape=[
            pltpu.VMEM((nop, bank.shape[3], bank.shape[2], bank.shape[4]), bank.dtype),
            pltpu.SMEM((nop,), jnp.int32),
        ],
        in_specs=[IN_HBM] * 3,
        out_specs=[WHOLE, IN_SMEM],
        scratch_shapes=[
            pltpu.SMEM((nop,), jnp.int32),
            pltpu.SMEM((nop,), jnp.int32),
            pltpu.VMEM(bank.shape, bank.dtype),
            pltpu.SemaphoreType.DMA((3,)),
        ],
        compiler_params=pltpu.CompilerParams(vmem_limit_bytes=VMEM_LIMIT),
        name="source_rows",
    )(*(pltpu.with_memory_space_constraint(x, pltpu.HBM) for x in (op_mom, op_disp, bank)))


def planar(matrices):
    return jnp.swapaxes(matrices, 1, 2)


def swap(array, masks, count):
    cores = len(masks)
    pairs = [(k * cores + c, (k ^ m) * cores + c) for k in range(count) for c, m in enumerate(masks)]
    return lax.ppermute(array, ("ta", "sa"), pairs)


def sink_kernel(entry_ref, forward_ref, own_ref, other_ref, out_ref, forward, rows, arrived):
    times, nop = rows.shape[:2]
    entries = [entry_ref[a] for a in range(nop)]
    whole = pltpu.make_async_copy(forward_ref, forward, arrived.at[nop])
    whole.start()
    copies = [
        pltpu.make_async_copy(own_ref.at[:, e], rows.at[:, a], arrived.at[a]) for a, e in enumerate(entries)
    ]
    for copy in copies:
        copy.start()
    mine = lax.axis_index("sa")

    def joined(matrices):
        split = [jnp.swapaxes(x, 0, 1) for x in matrices]
        return jnp.concatenate([jnp.concatenate([x[0], x[1]], axis=1) for x in split], axis=0)

    def multiply(half, lefts, rights):
        for t in range(times):
            out_ref[t, half] = lax.dot_general(
                lefts[t], rights[t], (((0,), (1,)), ((), ())), preferred_element_type=jnp.float32
            ).astype(jnp.bfloat16)

    rights = [joined([other_ref[t, e] for e in entries]) for t in range(times)]
    whole.wait()
    lefts = []
    for t in range(times):
        parts = jnp.swapaxes(forward[t, 0], 0, 1)
        for_real = jnp.concatenate([parts[0], -parts[1]], axis=0)
        for_imag = jnp.concatenate([parts[1], parts[0]], axis=0)
        lefts.append(jnp.concatenate([for_real, for_imag], axis=1))
    multiply(1 - mine, lefts, rights)
    for copy in copies:
        copy.wait()
    multiply(mine, lefts, [joined([rows[t, a] for a in range(nop)]) for t in range(times)])


def sink_products(forward, own_bank, other_bank, entries):
    nop = entries.shape[0]
    times, order = forward.shape[0], forward.shape[2]
    return pl.pallas_call(
        sink_kernel,
        out_shape=jax.ShapeDtypeStruct((times, 2, 2 * order, nop * own_bank.shape[2]), jnp.bfloat16),
        in_specs=[IN_SMEM, IN_HBM, IN_HBM, WHOLE],
        out_specs=WHOLE,
        scratch_shapes=[
            pltpu.VMEM(forward.shape, forward.dtype),
            pltpu.VMEM((times, nop) + own_bank.shape[2:], own_bank.dtype),
            pltpu.SemaphoreType.DMA((nop + 1,)),
        ],
        compiler_params=pltpu.CompilerParams(vmem_limit_bytes=VMEM_LIMIT),
        cost_estimate=pl.CostEstimate(
            flops=2 * times * 2 * order * 2 * order * order * nop,
            bytes_accessed=5 * 1024 * 1024,
            transcendentals=0,
        ),
        name="sink_product",
    )(
        pltpu.with_memory_space_constraint(entries, pltpu.SMEM),
        pltpu.with_memory_space_constraint(forward, pltpu.HBM),
        pltpu.with_memory_space_constraint(own_bank, pltpu.HBM),
        other_bank,
    )


def own_mask(masks, core):
    mask = masks[0]
    for c, m in enumerate(masks[1:], 1):
        mask = jnp.where(core == c, m, mask) if m != masks[0] else mask
    return mask


def sink_block(product_ref, t, start, nop, rows):
    order = product_ref.shape[2] // 2
    width = product_ref.shape[3] // nop
    parts = []
    for part in range(2):
        two = [product_ref[t, half, pl.ds(part * order + start, rows), :] for half in range(2)]
        parts.append(
            jnp.concatenate(
                [
                    jnp.concatenate([x[:, a * width : (a + 1) * width] for x in two], axis=1)
                    for a in range(nop)
                ],
                axis=0,
            )
        )
    return parts


def block_start(masks, rows, known):
    if known:
        return masks[0] * rows
    return pl.multiple_of((lax.axis_index("ta") ^ own_mask(masks, lax.axis_index("sa"))) * rows, rows)


def diagonal_sums(tables, nop, rows):
    width = nop * rows
    same = lax.broadcasted_iota(jnp.int32, (rows, width), 0) == lax.rem(
        lax.broadcasted_iota(jnp.int32, (rows, width), 1), rows
    )
    return jnp.concatenate(
        [jnp.where(same, x.reshape(nop, rows, width), 0.0) for x in tables], axis=0
    ).sum(axis=1)


def trace_kernel(masks, known, sums, nop, rows, *refs):
    product_ref, back_ref = refs[:2]
    piece_refs = refs[2 : 2 + len(masks)]
    before_ref = refs[2 + len(masks)] if len(refs) == 4 + len(masks) else None
    out_ref = refs[-1]
    times = product_ref.shape[0]
    order = back_ref.shape[2]
    totals = [None if before_ref is None else before_ref[t] for t in range(times)]
    nt = (((1,), (1,)), ((), ()))
    for mask, piece_ref in zip(masks, piece_refs):
        real, imag = (piece_ref[:, part].reshape(nop * rows, order) for part in range(2))
        for_real = jnp.concatenate([real, -imag], axis=1)
        for_imag = jnp.concatenate([imag, real], axis=1)
        left = jnp.concatenate([for_real, for_imag], axis=0)
        start = block_start(mask, rows, known)
        for t in range(times):
            reverse = jnp.dot(left, back_ref[t], preferred_element_type=jnp.float32)
            high = reverse.astype(jnp.bfloat16)
            low = (reverse - high.astype(jnp.float32)).astype(jnp.bfloat16)
            sink = jnp.concatenate(sink_block(product_ref, t, start, nop, rows), axis=0)
            added = lax.dot_general(sink, high, nt, preferred_element_type=jnp.float32)
            added += lax.dot_general(sink, low, nt, preferred_element_type=jnp.float32)
            totals[t] = added if totals[t] is None else totals[t] + added
    if not sums:
        for t in range(times):
            out_ref[t] = totals[t]
        return
    width = nop * rows
    tables = []
    for total in totals:
        (rr, ri), (ir, ii) = (
            [total[c * width : (c + 1) * width, d * width : (d + 1) * width] for d in range(2)] for c in range(2)
        )
        tables += [rr - ii, ri + ir]
    out_ref[...] = diagonal_sums(tables, nop, rows)


def traces(product, back, pieces, nop, rows, known=False, before=None, sums=False):
    times, order = product.shape[0], back.shape[2]
    side = 2 * nop * rows
    operands = [product, back, *pieces.values()] + ([] if before is None else [before])
    shape = (times * 2 * nop, nop * rows) if sums else (times, side, side)
    flops = 2 * times * len(pieces) * side * (2 * order * order + 2 * side * order)
    return pl.pallas_call(
        functools.partial(trace_kernel, tuple(pieces), known, sums, nop, rows),
        out_shape=jax.ShapeDtypeStruct(shape, jnp.float32),
        in_specs=[WHOLE] * len(operands),
        out_specs=WHOLE,
        compiler_params=pltpu.CompilerParams(vmem_limit_bytes=VMEM_LIMIT),
        cost_estimate=pl.CostEstimate(flops=flops, bytes_accessed=4 * 1024 * 1024, transcendentals=0),
        name="trace_sums" if sums else "traces",
    )(*operands)


def loop_kernel(masks, nop, rows, product_ref, back_ref, after_ref, out_ref):
    order = back_ref.shape[2]
    start = block_start(masks, rows, False)
    for t in range(product_ref.shape[0]):
        back = jnp.concatenate([back_ref[t, :order], back_ref[t, order:]], axis=1)
        real, imag = sink_block(product_ref, t, start, nop, rows)
        value = [
            lax.dot_general(x, back, (((1,), (1,)), ((), ())), preferred_element_type=jnp.float32)
            for x in (jnp.concatenate([real, -imag], axis=1), jnp.concatenate([imag, real], axis=1))
        ]
        for term in range(2):
            now = [x.astype(jnp.bfloat16) for x in value]
            value = [x - y.astype(jnp.float32) for x, y in zip(value, now)]
            out_ref[t, term, 0] = jnp.concatenate([now[0], -now[1]], axis=1)
            out_ref[t, term, 1] = jnp.concatenate([now[1], now[0]], axis=1)


def last_kernel(nop, rows, order, *refs):
    left_over = refs[0][...]
    out_ref = refs[-1]
    times = out_ref.shape[0]
    width = nop * rows
    if len(refs) > 2:
        piece_ref, loop_ref = refs[1:3]
        piece = jnp.concatenate([piece_ref[:, part].reshape(width, order) for part in range(2)], axis=1)
        met = loop_ref[...].reshape(-1, 2 * order)
        found = lax.dot_general(met, piece, (((1,), (1,)), ((), ())), preferred_element_type=jnp.float32)
        found = found.reshape(times, 2, 2, width, width)
        tables = [found[t, 0, part] + found[t, 1, part] for t in range(times) for part in range(2)]
        left_over = left_over + diagonal_sums(tables, nop, rows)
    height = left_over.shape[0]
    terms = []
    for _ in range(3):
        terms.append(left_over.astype(jnp.bfloat16))
        left_over = left_over - terms[-1].astype(jnp.float32)
    of_operator = (
        lax.broadcasted_iota(jnp.int32, (width, nop), 0) // rows
        == lax.broadcasted_iota(jnp.int32, (width, nop), 1)
    ).astype(jnp.bfloat16)
    paired = jnp.dot(jnp.concatenate(terms, axis=0), of_operator, preferred_element_type=jnp.float32)
    paired = (paired[:height] + (paired[height : 2 * height] + paired[2 * height :])) / order
    for t in range(times):
        for part in range(2):
            at = (2 * t + part) * nop
            out_ref[t, part] = paired[at : at + nop]


def finish(sums, nop, rows, order, *more):
    return pl.pallas_call(
        functools.partial(last_kernel, nop, rows, order),
        out_shape=jax.ShapeDtypeStruct((sums.shape[0] // (2 * nop), 2, nop, nop), jnp.float32),
        in_specs=[WHOLE] * (1 + len(more)),
        out_specs=WHOLE,
        compiler_params=pltpu.CompilerParams(vmem_limit_bytes=VMEM_LIMIT),
        name="traces_last",
    )(sums, *more)


def loops(product, back, after, masks, nop, rows):
    times, order = product.shape[0], back.shape[2]
    return pl.pallas_call(
        functools.partial(loop_kernel, masks, nop, rows),
        out_shape=jax.ShapeDtypeStruct((times, 2, 2, nop * rows, 2 * order), jnp.bfloat16),
        in_specs=[WHOLE, WHOLE, pl.BlockSpec(memory_space=pl.ANY)],
        out_specs=WHOLE,
        compiler_params=pltpu.CompilerParams(vmem_limit_bytes=VMEM_LIMIT),
        name="loops",
    )(product, back, after)


def per_device(forward, backward, sink_bank, source_bank, op_mom, op_disp, n_times):
    nop = op_mom.shape[0]
    order = forward.shape[2]
    times = forward.shape[0]
    own_rows = source_bank.shape[2]

    source, entries = chosen_source_rows(source_bank, op_mom, op_disp)
    other_bank = lax.ppermute(sink_bank, "sa", [(0, 1), (1, 0)])
    product = sink_products(
        forward,
        sink_bank,
        other_bank,
        entries,
    )
    back = planar(backward[0]).reshape(times, 2 * order, order)

    rows = order // (2 * nop)
    far_mask = n_times // 2
    if own_rows == rows and n_times == 2 * far_mask and far_mask & (far_mask - 1) == 0:
        near = tuple(range(1, far_mask))
        orders = (near[::-1], (near[1:-1] + near[:1] + near[-1:]))
        far = swap(source, (far_mask, far_mask), n_times)
        early = {(0, 0): source} | {m: swap(source, m, n_times) for m in zip(*orders)}
        early[far_mask, far_mask] = far
        far, product = lax.optimization_barrier((far, product))
        late = {(far_mask ^ m[0], far_mask ^ m[1]): swap(far, m, n_times) for m in zip(near, near[1:] + near[:1])}
        first = traces(product, back, early, nop, rows)
        last_masks = list(late)[-1]
        end = late.pop(last_masks)
        loop = loops(product, back, first, last_masks, nop, rows)
        sums = traces(product, back, late, nop, rows, before=first, sums=True)
        result = finish(sums, nop, rows, order, end, loop)
    else:
        whole = lax.all_gather(source, "ta", axis=2, tiled=True)
        pieces = {(k,): whole[:, :, k * rows : (k + 1) * rows] for k in range(order // rows)}
        sums = traces(product, back, pieces, nop, rows, known=True, sums=True)
        result = finish(sums, nop, rows, order)
    return result[:, None]


def solution(mesh):
    placed = (
        P(("cfg", "ta"), "sa", None, None, None),
        P(("cfg", "sa"), "ta", None, None, None),
        P(("cfg", "ta"), None, "sa", None, None),
        P(("cfg", "sa"), None, "ta", None, None),
        P(),
        P(),
    )
    return jax.shard_map(
        functools.partial(per_device, n_times=mesh.shape["ta"]),
        mesh=mesh,
        in_specs=placed,
        out_specs=P(("cfg", "ta"), "sa", None, None, None),
        check_vma=False,
    )
```
